256 devices in a mesh: dp: 16 (over z_hi, x, core), cent: 16 (over z_lo, y).
Axes of the slice: x: 4, y: 4, z: 8 (z_hi: 2, z_lo: 4; z = z_hi * 4 + z_lo), core: 2. Of those that a mesh axis runs over, the one named last changes fastest.
Arguments:
- points: bfloat16 [16384, 1024], P('dp'), may hold values from -6 to 6
- cent_one: bfloat16 [32768, 1024], P('cent'), may hold values from -6 to 6
- cent_two: bfloat16 [2048, 1024], replicated, may hold values from -6 to 6
Outputs:
- new_one: bfloat16 [32768, 1024], P('cent', 'dp')
- new_two: bfloat16 [2048, 1024], P(('dp', 'cent'))
The draws below stay inside these ranges and needn't reach their ends.
All inputs are finite; a program needn't handle non-finite values.
Results may differ from the reference program's by a relative error of at most 0.003.
Values may be sent and summed in bfloat16 or wider, within the bound.
No kernel may reach another device: no remote copies, remote signals or barrier semaphores. Data moves between devices by JAX's collectives and lax.ppermute only.
A program may use at most 64 MiB of HBM per device.

```python
import jax
import jax.numpy as jnp
from jax import lax

D = 1024
K1_DEV = 2048
K2 = 2048
PTS_DEV = 1024
NPTS = 16384
K1 = 32768


def rising_rows(count, rate):
    place = jnp.arange(count).astype(jnp.float32) / (count - 1)
    return jnp.sqrt(1.0 - place * (rate / jnp.sqrt(jnp.float32(D))))[:, None]


def draw_points(key, part):
    key = jax.random.fold_in(key, 1)
    values = jnp.clip(jax.random.normal(key, (NPTS, D), jnp.float32), -6.0, 6.0)
    return values.astype(jnp.bfloat16)


def draw_cent_one(key, part):
    key = jax.random.fold_in(key, 2)
    values = jnp.clip(jax.random.normal(key, (K1, D), jnp.float32) * rising_rows(K1, 4.0), -6.0, 6.0)
    return values.astype(jnp.bfloat16)


def draw_cent_two(key, part):
    key = jax.random.fold_in(key, 3)
    values = jnp.clip(0.3 * jax.random.normal(key, (K2, D), jnp.float32), -2.0, 2.0)
    return values.astype(jnp.bfloat16)


def setup_inputs(seed: int = 0) -> dict:
    seeds = jax.random.split(jax.random.key(seed), 4)
    points = draw_points(jax.random.fold_in(seeds[3], 71), 0)
    cent_one = draw_cent_one(jax.random.fold_in(seeds[3], 71), 0)
    cent_two = draw_cent_two(jax.random.fold_in(seeds[3], 71), 0)
    return {"points": points, "cent_one": cent_one, "cent_two": cent_two}


prior_one = 0.5
prior_two = 2.0
sharp_two = 0.25


def reference(points, cent_one, cent_two):
    sq_one = jnp.sum(jnp.square(cent_one.astype(jnp.float32)), axis=1)
    blocks = points.reshape(NPTS // PTS_DEV, PTS_DEV, D)

    def first_step(carry, block):
        numer, masses = carry
        scores = (2.0 * jnp.dot(block, cent_one.T, preferred_element_type=jnp.float32) - sq_one) * (0.5 * D ** -0.5)
        weights = jax.nn.softmax(scores, axis=1).astype(jnp.bfloat16)
        numer = numer + jnp.dot(weights.T, block, preferred_element_type=jnp.float32)
        masses = masses + jnp.sum(weights.astype(jnp.float32), axis=0)
        return (numer, masses), None

    start_one = (jnp.zeros((K1, D), jnp.float32), jnp.zeros((K1,), jnp.float32))
    (numer_one, mass_one), unused = lax.scan(first_step, start_one, blocks)
    new_one = ((numer_one + prior_one * cent_one.astype(jnp.float32)) / (mass_one[:, None] + prior_one)).astype(jnp.bfloat16)

    sq_two = jnp.sum(jnp.square(cent_two.astype(jnp.float32)), axis=1)
    rows_one = new_one.reshape(K1 // K1_DEV, K1_DEV, D)
    mass_rows = mass_one.reshape(K1 // K1_DEV, K1_DEV)

    def second_step(carry, pair):
        numer, masses = carry
        block, block_mass = pair
        second = (2.0 * jnp.dot(block, cent_two.T, preferred_element_type=jnp.float32) - sq_two) * sharp_two
        spread = (block_mass[:, None] * jax.nn.softmax(second, axis=1)).astype(jnp.bfloat16)
        numer = numer + jnp.dot(spread.T, block, preferred_element_type=jnp.float32)
        masses = masses + jnp.sum(spread.astype(jnp.float32), axis=0)
        return (numer, masses), None

    start_two = (jnp.zeros((K2, D), jnp.float32), jnp.zeros((K2,), jnp.float32))
    (numer_two, mass_two), unused = lax.scan(second_step, start_two, (rows_one, mass_rows))
    new_two = ((numer_two + prior_two * cent_two.astype(jnp.float32)) / (mass_two[:, None] + prior_two)).astype(jnp.bfloat16)
    return new_one, new_two
```

```python
import jax
import jax.numpy as jnp
from jax import lax
from jax.sharding import Mesh, PartitionSpec as P

prior_one = 0.5
prior_two = 2.0
sharp_two = 0.25

CENT = ("zl", "y")
OWN = ("core", "x", "zh")
ALL = ("zh", "x", "core", "zl", "y")
f32 = jnp.float32
bf16 = jnp.bfloat16


def swap(v, axis):
    return lax.all_to_all(v, axis, 0, 0, tiled=True)


def fold(v, axis, n):
    got = swap(v, axis).reshape((n, v.shape[0] // n) + v.shape[1:])
    return jnp.sum(got.astype(f32), axis=0)


def on_device(points, cent_one, cent_two):
    width = points.shape[1]
    local = cent_one.shape[0]
    count_two = cent_two.shape[0]
    n_pts = points.shape[0]

    with jax.named_scope("scores_one"):
        sq = jnp.sum(jnp.square(cent_one.astype(f32)), axis=1)
        inner = lax.dot_general(
            cent_one, points, (((1,), (1,)), ((), ())), preferred_element_type=f32
        )
        scores = (2.0 * inner - sq[:, None]) * (0.5 * width ** (-0.5))
        high = jnp.max(scores, axis=0)
        total = jnp.sum(jnp.exp(scores - high), axis=0)
    with jax.named_scope("exchange_softmax"):
        pair = jnp.concatenate([high, total])
        pairs = swap(jnp.broadcast_to(pair, (16, 2 * n_pts)), CENT)
        highs, totals = pairs[:, :n_pts], pairs[:, n_pts:]
        top = jnp.max(highs, axis=0)
        norm = top + jnp.log(jnp.sum(totals * jnp.exp(highs - top), axis=0))
    with jax.named_scope("sums_one"):
        weights = jnp.exp(scores - norm)
        mass_part = jnp.sum(weights, axis=1)
        numer = lax.dot_general(
            weights.astype(bf16), points, (((1,), (0,)), ((), ())), preferred_element_type=f32
        ).astype(bf16)
    with jax.named_scope("reduce_one"):
        mass = jnp.sum(swap(mass_part.reshape(16, local // 16), OWN), axis=0)
        part = fold(numer, "core", 2).astype(bf16)
        part = fold(part, "x", 4).astype(bf16)
        part = fold(part, "zh", 2)
    share = local // 16
    with jax.named_scope("finish_one"):
        place = (lax.axis_index("core") * 4 + lax.axis_index("x")) * 2 + lax.axis_index("zh")
        old = lax.dynamic_slice_in_dim(cent_one, place * share, share, 0).astype(f32)
        rows = ((part + prior_one * old) / (mass[:, None] + prior_one)).astype(bf16)
        out = rows.reshape(share, 2, 4, 2, width // 16).transpose(3, 2, 1, 0, 4)
        new_one = swap(out.reshape(16, share, width // 16), OWN).reshape(local, width // 16)
    with jax.named_scope("scores_two"):
        sq_two = jnp.sum(jnp.square(cent_two.astype(f32)), axis=1)
        inner = lax.dot_general(
            rows, cent_two, (((1,), (1,)), ((), ())), preferred_element_type=f32
        )
        second = (2.0 * inner - sq_two) * sharp_two
        spread = (mass[:, None] * jax.nn.softmax(second, axis=1)).astype(bf16)
        mass_two = jnp.sum(spread.astype(f32), axis=0)
        numer_two = lax.dot_general(
            spread, rows, (((0,), (0,)), ((), ())), preferred_element_type=f32
        ).astype(bf16)
    with jax.named_scope("reduce_two"):
        keep = count_two // 256

        def order(v):
            v = v.reshape((2, 4, 2, 4, 4, keep) + v.shape[1:])
            rest = tuple(range(6, v.ndim))
            v = v.transpose((2, 1, 4, 0, 3, 5) + rest)
            return v.reshape((count_two,) + v.shape[6:])

        part, mass = order(numer_two), order(mass_two)
        part, mass = fold(part, "core", 2).astype(bf16), fold(mass, "core", 2)
        part, mass = fold(part, "x", 4).astype(bf16), fold(mass, "x", 4)
        part, mass = fold(part, "y", 4), fold(mass, "y", 4)
        part, mass = fold(part, ("zh", "zl"), 8), fold(mass, ("zh", "zl"), 8)
    with jax.named_scope("finish_two"):
        place = lax.axis_index(ALL)
        old = lax.dynamic_slice_in_dim(cent_two, place * keep, keep, 0).astype(f32)
        new_two = ((part + prior_two * old) / (mass[:, None] + prior_two)).astype(bf16)
    return (new_one, new_two)


def solution(mesh):
    inner = Mesh(mesh.devices.reshape(2, 4, 2, 4, 4), ALL)
    dp = ("zh", "x", "core")
    in_specs = (P(dp, None), P(CENT, None), P())
    out_specs = (P(CENT, dp), P(ALL, None))
    return jax.shard_map(
        on_device, mesh=inner, in_specs=in_specs, out_specs=out_specs, check_vma=False
    )
```

```python
import functools

import jax
import jax.numpy as jnp
from jax import lax
from jax.experimental import pallas as pl
from jax.experimental.pallas import tpu as pltpu
from jax.sharding import Mesh, PartitionSpec as P

prior_one = 0.5
prior_two = 2.0
sharp_two = 0.25

CENT = ("zl", "y")
ALL = ("zh", "x", "core", "zl", "y")
HOPS = (2, 1, 3, 0)
EXTRA = 16
VMEM = 58 * 2**20
f32 = jnp.float32
bf16 = jnp.bfloat16


def swap(v, axis):
    return lax.all_to_all(v, axis, 0, 0, tiled=True)


def shift(v, axis, n, k):
    return lax.ppermute(v, axis, [(i, (i + k) % n) for i in range(n)])


def dot(a, b, dims):
    return lax.dot_general(a, b, (dims, ((), ())), preferred_element_type=f32)


def with_mass(v, block):
    mass = v[block : block + 1] + v[block + 1 : block + 2]
    rounded = lax.reduce_precision(mass, 8, 7)
    line = lax.broadcasted_iota(jnp.int32, v.shape, 0)
    v = jnp.where(line == block, rounded, jnp.where(line == block + 1, mass - rounded, v))
    return v.astype(bf16)


def log_total(scores):
    high = jnp.max(scores, axis=0)
    return high + jnp.log(jnp.sum(jnp.exp(scores - high), axis=0))


def sums_kernel(index, e_mine, e_other, f_mine, f_other, p_mine, p_other, *refs):
    outs, (acc, lanes, mass) = refs[:8], refs[8:]
    step = pl.program_id(0)
    half = pl.num_programs(0) // 2
    block = outs[0].shape[0] - EXTRA
    rows = 2 * block

    def add(e_ref, f_ref, p_ref, fresh):
        scale = f_ref[...]
        count = e_ref.shape[1]
        for i in range(4):
            at = slice(i * rows, (i + 1) * rows)
            w = e_ref[at, :].astype(f32) * scale
            lane = w[:, :128]
            for j in range(1, count // 128):
                lane = lane + w[:, j * 128 : (j + 1) * 128]
            part = dot(w.astype(bf16), p_ref[...], ((1,), (0,)))
            if fresh:
                lanes[at, :] = lane
                acc[at, :] = part
            else:
                lanes[at, :] += lane
                acc[at, :] += part

    @pl.when(step == 0)
    def first():
        add(e_mine, f_mine, p_mine, True)

    @pl.when((step > 0) & (step < half))
    def mine():
        add(e_mine, f_mine, p_mine, False)

    @pl.when(step >= half)
    def other():
        add(e_other, f_other, p_other, False)

    @pl.when(step == pl.num_programs(0) - 1)
    def finish():
        total = jnp.sum(lanes[...].T, axis=0, keepdims=True)
        for i in range(8):
            mass[i : i + 1, :] = total[:, i * block : (i + 1) * block]
        line = lax.broadcasted_iota(jnp.int32, (EXTRA, block), 0)
        for i, ref in enumerate(outs):
            at = index[i]
            ref[:block, :] = acc[pl.ds(pl.multiple_of(at * block, block), block), :].astype(ref.dtype)
            m = jnp.broadcast_to(mass[pl.ds(at, 1), :], (EXTRA, block))
            r = m.astype(ref.dtype).astype(f32)
            m = jnp.where(line == 0, r, jnp.where(line == 1, m - r, 0.0)).astype(ref.dtype)
            ref[block:, :] = jnp.concatenate([m] * (ref.shape[1] // block), axis=1)


def level_one_sums(index, e, factors, points):
    count, width = points[0].shape
    total = e[0].shape[0]
    block = total // 8
    steps = 4
    piece = 2 * count // steps
    low = lambda i: jnp.minimum(i, steps // 2 - 1)
    high = lambda i: jnp.maximum(i - steps // 2, 0)
    e_spec = lambda at: pl.BlockSpec((total, piece), lambda i, index: (0, at(i)))
    f_spec = lambda at: pl.BlockSpec((1, piece), lambda i, index: (0, at(i)))
    p_spec = lambda at: pl.BlockSpec((piece, width), lambda i, index: (at(i), 0))
    types = ([bf16] * 3 + [f32]) * 2
    return pl.pallas_call(
        sums_kernel,
        grid_spec=pltpu.PrefetchScalarGridSpec(
            num_scalar_prefetch=1,
            grid=(steps,),
            in_specs=[spec(at) for spec in (e_spec, f_spec, p_spec) for at in (low, high)],
            out_specs=[pl.BlockSpec((block + EXTRA, width), lambda i, index: (0, 0))] * 8,
            scratch_shapes=[
                pltpu.VMEM((total, width), f32),
                pltpu.VMEM((total, 128), f32),
                pltpu.VMEM((8, block), f32),
            ],
        ),
        out_shape=[jax.ShapeDtypeStruct((block + EXTRA, width), t) for t in types],
        compiler_params=pltpu.CompilerParams(vmem_limit_bytes=VMEM),
        cost_estimate=pl.CostEstimate(
            flops=4 * total * count * width,
            bytes_accessed=4 * count * (total + width) + 3 * total * width,
            transcendentals=0,
        ),
        name="level_one_sums",
    )(index, *e, *factors, *points)


def level_two_kernel(keep, core, rows_mine, rows_other, mass, table, out, rows, turned, second, spread):
    step = pl.program_id(0)
    block, width = rows_mine.shape
    piece = table.shape[0]
    steps = second.shape[0] // piece

    @pl.when(step == 0)
    def start():
        rows[:block, :width] = rows_mine[...]
        rows[block:, :width] = rows_other[...]
        rows[:, width:] = jnp.ones((2 * block, 128), bf16)
        turned[...] = rows[:, :width].astype(f32).T.astype(bf16)

    @pl.when(step < steps)
    def scores():
        wide = table[...].astype(f32)
        sq = jnp.sum(wide * wide, axis=1, keepdims=True) * sharp_two
        at = pl.multiple_of(step * piece, piece)
        second[pl.ds(at, piece), :] = (
            dot(table[...], turned[...], ((1,), (0,))) * (2.0 * sharp_two) - sq
        )

    @pl.when(step == steps)
    def softmax():
        high = jnp.max(second[...], axis=0, keepdims=True)
        e = jnp.exp(second[...] - high)
        second[...] = e
        weight = mass[...] / jnp.sum(e, axis=0, keepdims=True)
        for x in range(4):
            for y in range(4):
                starts = [
                    core[0] * (16 * keep) + ((zh * 4 + x) * 2 * 16 + zl * 4 + y) * keep
                    for zh in range(2)
                    for zl in range(4)
                ]
                v = [second[pl.ds(pl.multiple_of(s, keep), keep), :] for s in starts]
                to = (x * 4 + y) * 8 * keep
                spread[to : to + 8 * keep, :] = (jnp.concatenate(v) * weight).astype(bf16)

    @pl.when(step >= steps)
    def sums():
        count = out.shape[0]
        at = pl.multiple_of((step - steps) * count, count)
        v = dot(spread[pl.ds(at, count), :], rows[...], ((1,), (0,)))
        r = v.astype(bf16)
        out[:, :width] = r[:, :width]
        lane = lax.broadcasted_iota(jnp.int32, (count, 128), 1)
        left = (v[:, width:] - r[:, width:].astype(f32)).astype(bf16)
        out[:, width:] = jnp.where(lane > 0, left, r[:, width:])


def level_two_sums(core, rows_mine, rows_other, mass, table):
    block, width = rows_mine.shape
    count = table.shape[0]
    steps, writes = 8, 4
    whole = lambda shape: pl.BlockSpec(shape, lambda i, core: (0, 0))
    return pl.pallas_call(
        functools.partial(level_two_kernel, count // 256),
        grid_spec=pltpu.PrefetchScalarGridSpec(
            num_scalar_prefetch=1,
            grid=(steps + writes,),
            in_specs=[
                whole((block, width)),
                whole((block, width)),
                whole((1, 2 * block)),
                pl.BlockSpec((count // steps, width), lambda i, core: (jnp.minimum(i, steps - 1), 0)),
            ],
            out_specs=pl.BlockSpec(
                (count // 2 // writes, width + 128), lambda i, core: (jnp.maximum(i - steps, 0), 0)
            ),
            scratch_shapes=[
                pltpu.VMEM((2 * block, width + 128), bf16),
                pltpu.VMEM((width, 2 * block), bf16),
                pltpu.VMEM((count, 2 * block), f32),
                pltpu.VMEM((count // 2, 2 * block), bf16),
            ],
        ),
        out_shape=jax.ShapeDtypeStruct((count // 2, width + 128), bf16),
        compiler_params=pltpu.CompilerParams(vmem_limit_bytes=VMEM),
        cost_estimate=pl.CostEstimate(
            flops=8 * block * count * width,
            bytes_accessed=4 * count * width,
            transcendentals=2 * block * count,
        ),
        name="level_two_sums",
    )(core, rows_mine, rows_other, mass, table)


def on_device(points, cent_one, cent_two):
    width = points.shape[1]
    core, x, zh = lax.axis_index("core"), lax.axis_index("x"), lax.axis_index("zh")
    block = cent_one.shape[0] // 16

    scale = 0.5 * width ** (-0.5)

    with jax.named_scope("scores_one"):
        pts = (points, shift(points, "core", 2, 1))
        cents = lax.dynamic_slice_in_dim(cent_one, core * (8 * block), 8 * block, 0)
        sq = jnp.sum(jnp.square(cents.astype(f32)), axis=1)[:, None]

        def level_one_scores(p):
            scores = (2.0 * dot(cents, p, ((1,), (1,))) - sq) * scale
            high = jnp.max(scores, axis=0)
            e = jnp.exp(scores - high)
            return e.astype(bf16), high, high + jnp.log(jnp.sum(e, axis=0))

        first = level_one_scores(points)
        other, first = lax.optimization_barrier((pts[1], first))
        pts = (points, other)
        e, highs, sums = zip(first, level_one_scores(other))
    with jax.named_scope("exchange_softmax"):
        mine = log_total(jnp.stack([sums[0], shift(sums[1], "core", 2, 1)]))
        mine = log_total(swap(jnp.broadcast_to(mine, (16,) + mine.shape), CENT))
        norms = (mine, shift(mine, "core", 2, 1))
        factors = [jnp.exp(h - n)[None] for h, n in zip(highs, norms)]
    with jax.named_scope("reduce_one"):
        index = jnp.concatenate(
            [((x + jnp.array(HOPS, jnp.int32)) % 4) * 2 + part for part in (1 - zh, zh)]
        )
        parts = level_one_sums(index, e, factors, pts)
        sums = []
        for sent, own in ((parts[:3], parts[3]), (parts[4:7], parts[7])):
            got = [shift(v, "x", 4, k) for v, k in zip(sent, HOPS)]
            sums.append(own + sum(g.astype(f32) for g in got))
        part = sums[1] + lax.ppermute(with_mass(sums[0], block), "zh", [(0, 1), (1, 0)]).astype(f32)
    with jax.named_scope("finish_one"):
        mass = (part[block] + part[block + 1])[:block]
        place = ((core * 4 + x) * 2 + zh) * block
        old = lax.dynamic_slice_in_dim(cent_one, place, block, 0).astype(f32)
        rows = ((part[:block] + prior_one * old) / (mass[:, None] + prior_one)).astype(bf16)
        rows_other = shift(rows, "core", 2, 1)
        pairs = jnp.stack([mass, shift(mass, "core", 2, 1)])
        mass_all = pairs.reshape(1, 2 * block)
    with jax.named_scope("scores_two"):
        keep = cent_two.shape[0] // 256
        numer_two = level_two_sums(core.reshape(1), rows, rows_other, mass_all, cent_two)
    with jax.named_scope("out_one"):
        mine = [
            lax.dynamic_index_in_dim(r.reshape(block, 2, 4, 2, width // 16), core, 3, False)
            for r in (rows, rows_other)
        ]
        both = jnp.where(core == 0, jnp.stack(mine), jnp.stack(mine[::-1]))
        both = both.transpose(2, 3, 0, 1, 4)
        stay = lax.dynamic_index_in_dim(both, zh, 0, False)
        go = lax.dynamic_index_in_dim(both, 1 - zh, 0, False)
        come = lax.ppermute(go, "zh", [(0, 1), (1, 0)])
    with jax.named_scope("reduce_two"):
        part = swap(numer_two, ("x", "y")).reshape(16, 8 * keep, width + 128)
        part = jnp.sum(part.astype(f32), axis=0)
    with jax.named_scope("out_one"):
        pair = jnp.where(zh == 0, jnp.stack([stay, come]), jnp.stack([come, stay]))
        pair = pair.transpose(1, 0, 2, 3, 4)
        by_x = [lax.dynamic_index_in_dim(pair, (x + k) % 4, 0, False) for k in range(4)]
        by_x = jnp.stack([by_x[0]] + [shift(by_x[k], "x", 4, k) for k in (1, 2, 3)])
        by_x = jnp.roll(by_x[::-1], x + 1, axis=0)
        new_one = by_x.transpose(2, 0, 1, 3, 4).reshape(16 * block, width // 16)
    with jax.named_scope("reduce_two"):
        part = jnp.sum(swap(part, ("zh", "zl")).reshape(8, keep, width + 128), axis=0)
        mass = part[:, width : width + 1] + part[:, width + 1 : width + 2]
    with jax.named_scope("finish_two"):
        place = lax.axis_index(ALL)
        old = lax.dynamic_slice_in_dim(cent_two, place * keep, keep, 0).astype(f32)
        new_two = ((part[:, :width] + prior_two * old) / (mass + prior_two)).astype(bf16)
    return (new_one, new_two)


def solution(mesh):
    inner = Mesh(mesh.devices.reshape(2, 4, 2, 4, 4), ALL)
    dp = ("zh", "x", "core")
    in_specs = (P(dp, None), P(CENT, None), P())
    out_specs = (P(CENT, dp), P(ALL, None))
    return jax.shard_map(
        on_device, mesh=inner, in_specs=in_specs, out_specs=out_specs, check_vma=False
    )
```

```python
import functools

import jax
import jax.numpy as jnp
from jax import lax
from jax.experimental import pallas as pl
from jax.experimental.pallas import tpu as pltpu
from jax.sharding import Mesh, PartitionSpec as P

prior_one = 0.5
prior_two = 2.0
sharp_two = 0.25

CENT = ("zl", "y")
ALL = ("zh", "x", "core", "zl", "y")
HOPS = (2, 1, 3, 0)
EXTRA = 16
VMEM = 32 * 2**20
HBM = pl.BlockSpec(memory_space=pltpu.HBM)
f32 = jnp.float32
bf16 = jnp.bfloat16


def swap(v, axis):
    return lax.all_to_all(v, axis, 0, 0, tiled=True)


def shift(v, axis, n, k):
    return lax.ppermute(v, axis, [(i, (i + k) % n) for i in range(n)])


def far(v):
    return pltpu.with_memory_space_constraint(v, pltpu.HBM)


def dot(a, b, dims):
    return lax.dot_general(a, b, (dims, ((), ())), preferred_element_type=f32)


def with_mass(v, block):
    mass = v[block : block + 1] + v[block + 1 : block + 2]
    rounded = lax.reduce_precision(mass, 8, 7)
    line = lax.broadcasted_iota(jnp.int32, v.shape, 0)
    v = jnp.where(line == block, rounded, jnp.where(line == block + 1, mass - rounded, v))
    return v.astype(bf16)


def with_mass_columns(v, half):
    mass = v[:, half : half + 1] + v[:, half + 1 : half + 2]
    rounded = lax.reduce_precision(mass, 8, 7)
    lane = lax.broadcasted_iota(jnp.int32, v.shape, 1)
    v = jnp.where(lane == half, rounded, jnp.where(lane > half, mass - rounded, v))
    return v.astype(bf16)


def log_total(scores):
    high = jnp.max(scores, axis=0)
    return high + jnp.log(jnp.sum(jnp.exp(scores - high), axis=0))


def sums_kernel(index, e_mine, e_other, f_mine, f_other, p_mine, p_other, *refs):
    outs, (weights, lanes, e_held, p_held, e_sem, p_sem) = refs[:8], refs[8:]
    block = outs[0].shape[0] - EXTRA
    count, width = p_mine.shape
    e_copies, p_copies = [], []
    for i in range(8):
        at = pl.ds(pl.multiple_of(index[i] * block, block), block)
        for j, e in enumerate((e_mine, e_other)):
            e_copies.append(pltpu.make_async_copy(e.at[at, :], e_held.at[j, i], e_sem.at[j, i]))
    for j, p in enumerate((p_mine, p_other)):
        p_copies.append(pltpu.make_async_copy(p, p_held.at[j], p_sem.at[j]))
    for copy in e_copies + p_copies:
        copy.start()
    for i in range(8):
        to = slice(i * block, (i + 1) * block)
        lane = 0.0
        for j, f in enumerate((f_mine, f_other)):
            e_copies[2 * i + j].wait()
            w = e_held[j, i].astype(f32) * f[...]
            for n in range(count // 128):
                lane = lane + w[:, n * 128 : (n + 1) * 128]
            weights[to, j * count : (j + 1) * count] = w.astype(bf16)
        lanes[to, :] = lane
    mass = jnp.sum(lanes[...].T, axis=0, keepdims=True)
    line = lax.broadcasted_iota(jnp.int32, (EXTRA, block), 0)
    for copy in p_copies:
        copy.wait()
    for n in range(4):
        cols = slice(n * width // 4, (n + 1) * width // 4)
        v = dot(weights[:, :count], p_held[0, :, cols], ((1,), (0,)))
        v += dot(weights[:, count:], p_held[1, :, cols], ((1,), (0,)))
        for i, ref in enumerate(outs):
            ref[:block, cols] = v[i * block : (i + 1) * block, :].astype(ref.dtype)
    for i, ref in enumerate(outs):
        m = jnp.broadcast_to(mass[:, i * block : (i + 1) * block], (EXTRA, block))
        r = m.astype(ref.dtype).astype(f32)
        m = jnp.where(line == 0, r, jnp.where(line == 1, m - r, 0.0)).astype(ref.dtype)
        ref[block:, :] = jnp.concatenate([m] * (width // block), axis=1)


def level_one_sums(index, e, factors, points):
    count, width = points[0].shape
    total = e[0].shape[0]
    block = total // 8
    types = ([bf16] * 3 + [f32]) * 2
    vmem = pl.BlockSpec(memory_space=pltpu.VMEM)
    return pl.pallas_call(
        sums_kernel,
        in_specs=[pl.BlockSpec(memory_space=pltpu.SMEM)] + [HBM] * 2 + [vmem] * 2 + [HBM] * 2,
        out_specs=[vmem] * 8,
        scratch_shapes=[
            pltpu.VMEM((total, 2 * count), bf16),
            pltpu.VMEM((total, 128), f32),
            pltpu.VMEM((2, 8, block, count), bf16),
            pltpu.VMEM((2, count, width), bf16),
            pltpu.SemaphoreType.DMA((2, 8)),
            pltpu.SemaphoreType.DMA((2,)),
        ],
        out_shape=[jax.ShapeDtypeStruct((block + EXTRA, width), t) for t in types],
        compiler_params=pltpu.CompilerParams(vmem_limit_bytes=VMEM),
        cost_estimate=pl.CostEstimate(
            flops=4 * total * count * width,
            bytes_accessed=4 * count * (total + width) + 3 * total * width,
            transcendentals=0,
        ),
        name="level_one_sums",
    )(index, *map(far, e), *factors, *map(far, points))


def level_two_kernel(
    keep, place, rows_mine, rows_other, mass, table_far, *refs
):
    outs, (rows, turned, second, spread, table, sem) = refs[:8], refs[8:]
    block, width = rows_mine.shape
    count = table.shape[0]
    pieces = [slice(i * count // 4, (i + 1) * count // 4) for i in range(4)]
    copies = [
        pltpu.make_async_copy(table_far.at[at, :], table.at[at, :], sem.at[i])
        for i, at in enumerate(pieces)
    ]
    for copy in copies:
        copy.start()
    rows[:block, :width] = rows_mine[...]
    rows[block:, :width] = rows_other[...]
    rows[:, width:] = jnp.ones((2 * block, 128), bf16)
    turned[...] = rows[:, :width].astype(f32).T.astype(bf16)
    high = jnp.full((1, 2 * block), -jnp.inf, f32)
    for copy, at in zip(copies, pieces):
        copy.wait()
        wide = table[at, :].astype(f32)
        sq = jnp.sum(wide * wide, axis=1, keepdims=True) * sharp_two
        v = dot(table[at, :], turned[...], ((1,), (0,))) * (2.0 * sharp_two) - sq
        second[at, :] = v
        high = jnp.maximum(high, jnp.max(v, axis=0, keepdims=True))
    total = jnp.zeros((1, 2 * block), f32)
    for at in pieces:
        v = jnp.exp(second[at, :] - high)
        second[at, :] = v
        total = total + jnp.sum(v, axis=0, keepdims=True)
    weight = mass[...] / total
    half = width // 2
    lane = lax.broadcasted_iota(jnp.int32, (8 * 4 * keep, 128), 1)
    for i in range(4):
        for color in range(2):
            for j in range(4):
                to_x, to_y = (i, j) if color == 0 else (j, i)
                start = place[0] + (place[1 + to_x] * 32 + place[5 + to_y]) * keep
                starts = [start + (zh * 128 + zl * 4) * keep for zh in range(2) for zl in range(4)]
                v = [second[pl.ds(pl.multiple_of(s, keep), keep), :] for s in starts]
                to = slice(j * 8 * keep, (j + 1) * 8 * keep)
                spread[2 * i + color, to, :] = (jnp.concatenate(v) * weight).astype(bf16)
            cols = slice(0, half) if color == 0 else slice(half, width + 128)
            v = dot(spread[2 * i + color], rows[:, cols], ((1,), (0,)))
            out = outs[4 * color + i]
            if color == 0:
                out[...] = v.astype(out.dtype)
                continue
            r = v.astype(out.dtype)
            out[:, :half] = r[:, :half]
            left = (v[:, half:] - r[:, half:].astype(f32)).astype(out.dtype)
            out[:, half:] = jnp.where(lane > 0, left, r[:, half:])


def level_two_sums(place, rows_mine, rows_other, mass, table):
    block, width = rows_mine.shape
    count = table.shape[0]
    vmem = pl.BlockSpec(memory_space=pltpu.VMEM)
    return pl.pallas_call(
        functools.partial(level_two_kernel, count // 256),
        in_specs=[pl.BlockSpec(memory_space=pltpu.SMEM)] + [vmem] * 3 + [HBM],
        out_specs=[vmem] * 8,
        scratch_shapes=[
            pltpu.VMEM((2 * block, width + 128), bf16),
            pltpu.VMEM((width, 2 * block), bf16),
            pltpu.VMEM((count, 2 * block), f32),
            pltpu.VMEM((8, count // 8, 2 * block), bf16),
            pltpu.VMEM((count, width), bf16),
            pltpu.SemaphoreType.DMA((4,)),
        ],
        out_shape=[
            jax.ShapeDtypeStruct((count // 8, cols), t)
            for cols in (width // 2, width // 2 + 128)
            for t in (bf16, bf16, bf16, f32)
        ],
        compiler_params=pltpu.CompilerParams(vmem_limit_bytes=VMEM),
        cost_estimate=pl.CostEstimate(
            flops=8 * block * count * width,
            bytes_accessed=4 * count * width,
            transcendentals=2 * block * count,
        ),
        name="level_two_sums",
    )(place, rows_mine, rows_other, mass, far(table))


def on_device(points, cent_one, cent_two):
    width = points.shape[1]
    core, x, y, zh = [lax.axis_index(name) for name in ("core", "x", "y", "zh")]
    block = cent_one.shape[0] // 16

    scale = 0.5 * width ** (-0.5)

    with jax.named_scope("scores_one"):
        pts = (points, shift(points, "core", 2, 1))
        cents = lax.dynamic_slice_in_dim(cent_one, core * (8 * block), 8 * block, 0)
        sq = jnp.sum(jnp.square(cents.astype(f32)), axis=1)[:, None]

        def level_one_scores(p):
            scores = (2.0 * dot(cents, p, ((1,), (1,))) - sq) * scale
            high = jnp.max(scores, axis=0)
            e = jnp.exp(scores - high)
            return e.astype(bf16), high, high + jnp.log(jnp.sum(e, axis=0))

        first = level_one_scores(points)
        other, first = lax.optimization_barrier((pts[1], first))
        pts = (points, other)
        e, highs, sums = zip(first, level_one_scores(other))
    with jax.named_scope("exchange_softmax"):
        mine = log_total(jnp.stack([sums[0], shift(sums[1], "core", 2, 1)]))
        mine = log_total(swap(jnp.broadcast_to(mine, (16,) + mine.shape), CENT))
        norms = (mine, shift(mine, "core", 2, 1))
        factors = [jnp.exp(h - n)[None] for h, n in zip(highs, norms)]
    with jax.named_scope("reduce_one"):
        index = jnp.concatenate(
            [((x + jnp.array(HOPS, jnp.int32)) % 4) * 2 + part for part in (1 - zh, zh)]
        )
        parts = level_one_sums(index, e, factors, pts)
        sums = []
        for sent, own in ((parts[:3], parts[3]), (parts[4:7], parts[7])):
            got = [shift(v, "x", 4, k) for v, k in zip(sent, HOPS)]
            sums.append(own + sum(g.astype(f32) for g in got))
        part = sums[1] + lax.ppermute(with_mass(sums[0], block), "zh", [(0, 1), (1, 0)]).astype(f32)
    with jax.named_scope("finish_one"):
        mass = (part[block] + part[block + 1])[:block]
        place = ((core * 4 + x) * 2 + zh) * block
        old = lax.dynamic_slice_in_dim(cent_one, place, block, 0).astype(f32)
        rows = ((part[:block] + prior_one * old) / (mass[:, None] + prior_one)).astype(bf16)
        rows_other = shift(rows, "core", 2, 1)
        mass_all = jnp.stack([mass, shift(mass, "core", 2, 1)]).reshape(1, 2 * block)
    with jax.named_scope("scores_two"):
        keep = cent_two.shape[0] // 256
        hops = jnp.array(HOPS, jnp.int32)
        place = jnp.concatenate([(core * 16 * keep).reshape(1), (x + hops) % 4, (y + hops) % 4])
        parts = level_two_sums(place, rows, rows_other, mass_all, cent_two)
    with jax.named_scope("reduce_two"):
        half = width // 2
        size = 8 * keep

        def gather(parts, axis):
            got = [shift(v, axis, 4, k) for v, k in zip(parts[:3], HOPS)]
            return parts[3] + sum(g.astype(f32) for g in got)

        one, two = gather(parts[:4], "x"), gather(parts[4:], "y")
        cut = lambda v: [v[i * size : (i + 1) * size] for i in range(3)]
        one = gather(cut(one.astype(bf16)) + [one[3 * size :]], "y")
        two = gather(cut(with_mass_columns(two, half)) + [two[3 * size :]], "x")
        part = wide = jnp.concatenate([one, two], axis=1)
        part = jnp.sum(swap(part, ("zh", "zl")).reshape(8, keep, width + 128), axis=0)
        mass = part[:, width : width + 1] + part[:, width + 1 : width + 2]
    with jax.named_scope("out_one"):
        mine = [
            lax.dynamic_index_in_dim(r.reshape(block, 2, 4, 2, width // 16), core, 3, False)
            for r in (rows, rows_other)
        ]
        both = jnp.where(core == 0, jnp.stack(mine), jnp.stack(mine[::-1]))
        both = both.transpose(2, 3, 0, 1, 4)
        stay = lax.dynamic_index_in_dim(both, zh, 0, False)
        go = lax.dynamic_index_in_dim(both, 1 - zh, 0, False)
        come = lax.ppermute(go, "zh", [(0, 1), (1, 0)])
        pair = jnp.where(zh == 0, jnp.stack([stay, come]), jnp.stack([come, stay]))
        pair = pair.transpose(1, 0, 2, 3, 4)
        by_x = [lax.dynamic_index_in_dim(pair, (x + k) % 4, 0, False) for k in range(4)]
        by_x, _ = lax.optimization_barrier((by_x, wide))
        by_x = jnp.stack([by_x[0]] + [shift(by_x[k], "x", 4, k) for k in (1, 2, 3)])
        by_x = jnp.roll(by_x[::-1], x + 1, axis=0)
        new_one = by_x.transpose(2, 0, 1, 3, 4).reshape(16 * block, width // 16)
    with jax.named_scope("finish_two"):
        place = lax.axis_index(ALL)
        old = lax.dynamic_slice_in_dim(cent_two, place * keep, keep, 0).astype(f32)
        new_two = ((part[:, :width] + prior_two * old) / (mass + prior_two)).astype(bf16)
    return (new_one, new_two)


def solution(mesh):
    inner = Mesh(mesh.devices.reshape(2, 4, 2, 4, 4), ALL)
    dp = ("zh", "x", "core")
    in_specs = (P(dp, None), P(CENT, None), P())
    out_specs = (P(CENT, dp), P(ALL, None))
    return jax.shard_map(
        on_device, mesh=inner, in_specs=in_specs, out_specs=out_specs, check_vma=False
    )
```

```python
import functools

import jax
import jax.numpy as jnp
from jax import lax
from jax.experimental import pallas as pl
from jax.experimental.pallas import tpu as pltpu
from jax.sharding import Mesh, PartitionSpec as P

prior_one = 0.5
prior_two = 2.0
sharp_two = 0.25

CENT = ("zl", "y")
ALL = ("zh", "x", "core", "zl", "y")
HOPS = (2, 1, 3, 0)
EXTRA = 16
VMEM = 32 * 2**20
HBM = pl.BlockSpec(memory_space=pltpu.HBM)
f32 = jnp.float32
bf16 = jnp.bfloat16


def swap(v, axis):
    return lax.all_to_all(v, axis, 0, 0, tiled=True)


def shift(v, axis, n, k):
    return lax.ppermute(v, axis, [(i, (i + k) % n) for i in range(n)])


def far(v):
    return pltpu.with_memory_space_constraint(v, pltpu.HBM)


def dot(a, b, dims):
    return lax.dot_general(a, b, (dims, ((), ())), preferred_element_type=f32)


def with_mass(v, block):
    mass = v[block : block + 1] + v[block + 1 : block + 2]
    rounded = lax.reduce_precision(mass, 8, 7)
    line = lax.broadcasted_iota(jnp.int32, v.shape, 0)
    v = jnp.where(line == block, rounded, jnp.where(line == block + 1, mass - rounded, v))
    return v.astype(bf16)


def with_mass_columns(v, half):
    mass = v[:, half : half + 1] + v[:, half + 1 : half + 2]
    rounded = lax.reduce_precision(mass, 8, 7)
    lane = lax.broadcasted_iota(jnp.int32, v.shape, 1)
    v = jnp.where(lane == half, rounded, jnp.where(lane > half, mass - rounded, v))
    return v.astype(bf16)


def log_total(scores):
    high = jnp.max(scores, axis=0)
    return high + jnp.log(jnp.sum(jnp.exp(scores - high), axis=0))


def sums_kernel(index, e_mine, e_other, f_mine, f_other, p_mine, p_other, *refs):
    outs, (weights, lanes, e_held, p_held, e_sem, p_sem) = refs[:4], refs[4:]
    block = outs[0].shape[0] - EXTRA
    count, width = p_mine.shape
    e_copies, p_copies = [], []
    for i in range(4):
        at = pl.ds(pl.multiple_of(index[i] * block, block), block)
        for j, e in enumerate((e_mine, e_other)):
            e_copies.append(pltpu.make_async_copy(e.at[at, :], e_held.at[j, i], e_sem.at[j, i]))
    for j, p in enumerate((p_mine, p_other)):
        p_copies.append(pltpu.make_async_copy(p, p_held.at[j], p_sem.at[j]))
    for copy in e_copies + p_copies:
        copy.start()
    for i in range(4):
        to = slice(i * block, (i + 1) * block)
        lane = 0.0
        for j, f in enumerate((f_mine, f_other)):
            e_copies[2 * i + j].wait()
            w = e_held[j, i].astype(f32) * f[...]
            for n in range(count // 128):
                lane = lane + w[:, n * 128 : (n + 1) * 128]
            weights[to, j * count : (j + 1) * count] = w.astype(bf16)
        lanes[to, :] = lane
    mass = jnp.sum(lanes[...].T, axis=0, keepdims=True)
    line = lax.broadcasted_iota(jnp.int32, (EXTRA, block), 0)
    for copy in p_copies:
        copy.wait()
    for n in range(4):
        cols = slice(n * width // 4, (n + 1) * width // 4)
        v = dot(weights[:, :count], p_held[0, :, cols], ((1,), (0,)))
        v += dot(weights[:, count:], p_held[1, :, cols], ((1,), (0,)))
        for i, ref in enumerate(outs):
            ref[:block, cols] = v[i * block : (i + 1) * block, :].astype(ref.dtype)
    for i, ref in enumerate(outs):
        m = jnp.broadcast_to(mass[:, i * block : (i + 1) * block], (EXTRA, block))
        r = m.astype(ref.dtype).astype(f32)
        m = jnp.where(line == 0, r, jnp.where(line == 1, m - r, 0.0)).astype(ref.dtype)
        ref[block:, :] = jnp.concatenate([m] * (width // block), axis=1)


def level_one_sums(index, e, factors, points):
    count, width = points[0].shape
    total = e[0].shape[0]
    block = total // 8
    types = [bf16] * 3 + [f32]
    vmem = pl.BlockSpec(memory_space=pltpu.VMEM)
    return pl.pallas_call(
        sums_kernel,
        in_specs=[pl.BlockSpec(memory_space=pltpu.SMEM)] + [HBM] * 2 + [vmem] * 2 + [HBM] * 2,
        out_specs=[vmem] * 4,
        scratch_shapes=[
            pltpu.VMEM((4 * block, 2 * count), bf16),
            pltpu.VMEM((4 * block, 128), f32),
            pltpu.VMEM((2, 4, block, count), bf16),
            pltpu.VMEM((2, count, width), bf16),
            pltpu.SemaphoreType.DMA((2, 4)),
            pltpu.SemaphoreType.DMA((2,)),
        ],
        out_shape=[jax.ShapeDtypeStruct((block + EXTRA, width), t) for t in types],
        compiler_params=pltpu.CompilerParams(vmem_limit_bytes=VMEM),
        cost_estimate=pl.CostEstimate(
            flops=2 * total * count * width,
            bytes_accessed=2 * count * (total + 2 * width) + 2 * total * width,
            transcendentals=0,
        ),
        name="level_one_sums",
    )(index, *map(far, e), *factors, *map(far, points))


def level_two_kernel(
    keep, place, rows_mine, rows_other, mass, table_far, *refs
):
    outs, (rows, turned, second, spread, table, sem) = refs[:8], refs[8:]
    block, width = rows_mine.shape
    count = table.shape[0]
    pieces = [slice(i * count // 4, (i + 1) * count // 4) for i in range(4)]
    copies = [
        pltpu.make_async_copy(table_far.at[at, :], table.at[at, :], sem.at[i])
        for i, at in enumerate(pieces)
    ]
    for copy in copies:
        copy.start()
    rows[:block, :width] = rows_mine[...]
    rows[block:, :width] = rows_other[...]
    rows[:, width:] = jnp.ones((2 * block, 128), bf16)
    turned[...] = rows[:, :width].astype(f32).T.astype(bf16)
    high = jnp.full((1, 2 * block), -jnp.inf, f32)
    for copy, at in zip(copies, pieces):
        copy.wait()
        wide = table[at, :].astype(f32)
        sq = jnp.sum(wide * wide, axis=1, keepdims=True) * sharp_two
        v = dot(table[at, :], turned[...], ((1,), (0,))) * (2.0 * sharp_two) - sq
        second[at, :] = v
        high = jnp.maximum(high, jnp.max(v, axis=0, keepdims=True))
    total = jnp.zeros((1, 2 * block), f32)
    for at in pieces:
        v = jnp.exp(second[at, :] - high)
        second[at, :] = v
        total = total + jnp.sum(v, axis=0, keepdims=True)
    weight = mass[...] / total
    half = width // 2
    lane = lax.broadcasted_iota(jnp.int32, (8 * 4 * keep, 128), 1)
    for i in range(4):
        for color in range(2):
            for j in range(4):
                to_x, to_y = (i, j) if color == 0 else (j, i)
                start = place[0] + (place[1 + to_x] * 32 + place[5 + to_y]) * keep
                starts = [start + (zh * 128 + zl * 4) * keep for zh in range(2) for zl in range(4)]
                v = [second[pl.ds(pl.multiple_of(s, keep), keep), :] for s in starts]
                to = slice(j * 8 * keep, (j + 1) * 8 * keep)
                spread[2 * i + color, to, :] = (jnp.concatenate(v) * weight).astype(bf16)
            cols = slice(0, half) if color == 0 else slice(half, width + 128)
            v = dot(spread[2 * i + color], rows[:, cols], ((1,), (0,)))
            out = outs[4 * color + i]
            if color == 0:
                out[...] = v.astype(out.dtype)
                continue
            r = v.astype(out.dtype)
            out[:, :half] = r[:, :half]
            left = (v[:, half:] - r[:, half:].astype(f32)).astype(out.dtype)
            out[:, half:] = jnp.where(lane > 0, left, r[:, half:])


def level_two_sums(place, rows_mine, rows_other, mass, table):
    block, width = rows_mine.shape
    count = table.shape[0]
    vmem = pl.BlockSpec(memory_space=pltpu.VMEM)
    return pl.pallas_call(
        functools.partial(level_two_kernel, count // 256),
        in_specs=[pl.BlockSpec(memory_space=pltpu.SMEM)] + [vmem] * 3 + [HBM],
        out_specs=[vmem] * 8,
        scratch_shapes=[
            pltpu.VMEM((2 * block, width + 128), bf16),
            pltpu.VMEM((width, 2 * block), bf16),
            pltpu.VMEM((count, 2 * block), f32),
            pltpu.VMEM((8, count // 8, 2 * block), bf16),
            pltpu.VMEM((count, width), bf16),
            pltpu.SemaphoreType.DMA((4,)),
        ],
        out_shape=[
            jax.ShapeDtypeStruct((count // 8, cols), t)
            for cols in (width // 2, width // 2 + 128)
            for t in (bf16, bf16, bf16, f32)
        ],
        compiler_params=pltpu.CompilerParams(vmem_limit_bytes=VMEM),
        cost_estimate=pl.CostEstimate(
            flops=8 * block * count * width,
            bytes_accessed=4 * count * width,
            transcendentals=2 * block * count,
        ),
        name="level_two_sums",
    )(place, rows_mine, rows_other, mass, far(table))


def on_device(points, cent_one, cent_two):
    width = points.shape[1]
    core, x, y, zh = [lax.axis_index(name) for name in ("core", "x", "y", "zh")]
    block = cent_one.shape[0] // 16

    scale = 0.5 * width ** (-0.5)

    with jax.named_scope("scores_one"):
        pts = (points, shift(points, "core", 2, 1))
        cents = lax.dynamic_slice_in_dim(cent_one, core * (8 * block), 8 * block, 0)
        sq = jnp.sum(jnp.square(cents.astype(f32)), axis=1)[:, None]

        def level_one_scores(p):
            scores = (2.0 * dot(cents, p, ((1,), (1,))) - sq) * scale
            high = jnp.max(scores, axis=0)
            e = jnp.exp(scores - high)
            return e.astype(bf16), high, high + jnp.log(jnp.sum(e, axis=0))

        first = level_one_scores(points)
        other, first = lax.optimization_barrier((pts[1], first))
        pts = (points, other)
        e, highs, sums = zip(first, level_one_scores(other))
    with jax.named_scope("exchange_softmax"):
        mine = log_total(jnp.stack([sums[0], shift(sums[1], "core", 2, 1)]))
        mine = log_total(swap(jnp.broadcast_to(mine, (16,) + mine.shape), CENT))
        norms = (mine, shift(mine, "core", 2, 1))
        factors = [jnp.exp(h - n)[None] for h, n in zip(highs, norms)]
    with jax.named_scope("reduce_one"):
        sums = []
        for z in (1 - zh, zh):
            index = ((x + jnp.array(HOPS, jnp.int32)) % 4) * 2 + z
            *sent, own = level_one_sums(index, e, factors, pts)
            got = [shift(v, "x", 4, k) for v, k in zip(sent, HOPS)]
            sums.append(own + sum(g.astype(f32) for g in got))
        part = sums[1] + lax.ppermute(with_mass(sums[0], block), "zh", [(0, 1), (1, 0)]).astype(f32)
    with jax.named_scope("finish_one"):
        mass = (part[block] + part[block + 1])[:block]
        place = ((core * 4 + x) * 2 + zh) * block
        old = lax.dynamic_slice_in_dim(cent_one, place, block, 0).astype(f32)
        rows = ((part[:block] + prior_one * old) / (mass[:, None] + prior_one)).astype(bf16)
        rows_other = shift(rows, "core", 2, 1)
        mass_all = jnp.stack([mass, shift(mass, "core", 2, 1)]).reshape(1, 2 * block)
    with jax.named_scope("scores_two"):
        keep = cent_two.shape[0] // 256
        hops = jnp.array(HOPS, jnp.int32)
        place = jnp.concatenate([(core * 16 * keep).reshape(1), (x + hops) % 4, (y + hops) % 4])
        parts = level_two_sums(place, rows, rows_other, mass_all, cent_two)
    with jax.named_scope("reduce_two"):
        half = width // 2
        size = 8 * keep

        def gather(parts, axis):
            got = [shift(v, axis, 4, k) for v, k in zip(parts[:3], HOPS)]
            return parts[3] + sum(g.astype(f32) for g in got)

        one, two = gather(parts[:4], "x"), gather(parts[4:], "y")
        cut = lambda v: [v[i * size : (i + 1) * size] for i in range(3)]
        one = gather(cut(one.astype(bf16)) + [one[3 * size :]], "y")
        two = gather(cut(with_mass_columns(two, half)) + [two[3 * size :]], "x")
        part = wide = jnp.concatenate([one, two], axis=1)
        part = jnp.sum(swap(part, ("zh", "zl")).reshape(8, keep, width + 128), axis=0)
        mass = part[:, width : width + 1] + part[:, width + 1 : width + 2]
    with jax.named_scope("out_one"):
        mine = [
            lax.dynamic_index_in_dim(r.reshape(block, 2, 4, 2, width // 16), core, 3, False)
            for r in (rows, rows_other)
        ]
        both = jnp.where(core == 0, jnp.stack(mine), jnp.stack(mine[::-1]))
        both = both.transpose(2, 3, 0, 1, 4)
        stay = lax.dynamic_index_in_dim(both, zh, 0, False)
        go = lax.dynamic_index_in_dim(both, 1 - zh, 0, False)
        come = lax.ppermute(go, "zh", [(0, 1), (1, 0)])
        pair = jnp.where(zh == 0, jnp.stack([stay, come]), jnp.stack([come, stay]))
        pair = pair.transpose(1, 0, 2, 3, 4)
        by_x = [lax.dynamic_index_in_dim(pair, (x + k) % 4, 0, False) for k in range(4)]
        by_x, _ = lax.optimization_barrier((by_x, wide))
        by_x = jnp.stack([by_x[0]] + [shift(by_x[k], "x", 4, k) for k in (1, 2, 3)])
        by_x = jnp.roll(by_x[::-1], x + 1, axis=0)
        new_one = by_x.transpose(2, 0, 1, 3, 4).reshape(16 * block, width // 16)
    with jax.named_scope("finish_two"):
        place = lax.axis_index(ALL)
        old = lax.dynamic_slice_in_dim(cent_two, place * keep, keep, 0).astype(f32)
        new_two = ((part[:, :width] + prior_two * old) / (mass + prior_two)).astype(bf16)
    return (new_one, new_two)


def solution(mesh):
    inner = Mesh(mesh.devices.reshape(2, 4, 2, 4, 4), ALL)
    dp = ("zh", "x", "core")
    in_specs = (P(dp, None), P(CENT, None), P())
    out_specs = (P(CENT, dp), P(ALL, None))
    return jax.shard_map(
        on_device, mesh=inner, in_specs=in_specs, out_specs=out_specs, check_vma=False
    )
```

```python
import functools

import jax
import jax.numpy as jnp
from jax import lax
from jax.experimental import pallas as pl
from jax.experimental.pallas import tpu as pltpu
from jax.sharding import Mesh, PartitionSpec as P

prior_one = 0.5
prior_two = 2.0
sharp_two = 0.25

CENT = ("zl", "y")
ALL = ("zh", "x", "core", "zl", "y")
HOPS = (2, 1, 3, 0)
EXTRA = 16
VMEM = 32 * 2**20
HBM = pl.BlockSpec(memory_space=pltpu.HBM)
f32 = jnp.float32
bf16 = jnp.bfloat16


def swap(v, axis):
    return lax.all_to_all(v, axis, 0, 0, tiled=True)


def shift(v, axis, n, k):
    return lax.ppermute(v, axis, [(i, (i + k) % n) for i in range(n)])


def far(v):
    return pltpu.with_memory_space_constraint(v, pltpu.HBM)


def dot(a, b, dims):
    return lax.dot_general(a, b, (dims, ((), ())), preferred_element_type=f32)


def with_mass(v, block):
    mass = v[block : block + 1] + v[block + 1 : block + 2]
    rounded = lax.reduce_precision(mass, 8, 7)
    line = lax.broadcasted_iota(jnp.int32, v.shape, 0)
    v = jnp.where(line == block, rounded, jnp.where(line == block + 1, mass - rounded, v))
    return v.astype(bf16)


def with_mass_columns(v, half):
    mass = v[:, half : half + 1] + v[:, half + 1 : half + 2]
    rounded = lax.reduce_precision(mass, 8, 7)
    lane = lax.broadcasted_iota(jnp.int32, v.shape, 1)
    v = jnp.where(lane == half, rounded, jnp.where(lane > half, mass - rounded, v))
    return v.astype(bf16)


def log_total(scores):
    high = jnp.max(scores, axis=0)
    return high + jnp.log(jnp.sum(jnp.exp(scores - high), axis=0))


def sums_kernel(index, e_mine, e_other, f_mine, f_other, p_mine, p_other, *refs):
    outs, (weights, lanes, e_held, p_held, e_sem, p_sem) = refs[:4], refs[4:]
    block = outs[0].shape[0] - EXTRA
    count, width = p_mine.shape
    def e_copy(i, j, e):
        at = pl.ds(pl.multiple_of(index[i] * block, block), block)
        return pltpu.make_async_copy(e.at[at, :], e_held.at[j, i], e_sem.at[j, i])

    p_copies = [
        pltpu.make_async_copy(p, p_held.at[j], p_sem.at[j]) for j, p in enumerate((p_mine, p_other))
    ]
    for i in range(4):
        for j, e in enumerate((e_mine, e_other)):
            e_copy(i, j, e).start()
    for copy in p_copies:
        copy.start()

    def fill(i, carry):
        to = pl.ds(pl.multiple_of(i * block, block), block)
        lane = 0.0
        for j, (e, f) in enumerate(((e_mine, f_mine), (e_other, f_other))):
            e_copy(i, j, e).wait()
            w = e_held[j, i].astype(f32) * f[...]
            for n in range(count // 128):
                lane = lane + w[:, n * 128 : (n + 1) * 128]
            weights[to, j * count : (j + 1) * count] = w.astype(bf16)
        lanes[to, :] = lane
        return carry

    lax.fori_loop(0, 4, fill, 0)
    mass = jnp.sum(lanes[...].T, axis=0, keepdims=True)
    line = lax.broadcasted_iota(jnp.int32, (EXTRA, block), 0)
    for copy in p_copies:
        copy.wait()

    def tile(n, carry):
        cols = pl.ds(pl.multiple_of(n * (width // 4), width // 4), width // 4)
        v = dot(weights[:, :count], p_held[0, :, cols], ((1,), (0,)))
        v += dot(weights[:, count:], p_held[1, :, cols], ((1,), (0,)))
        for i, ref in enumerate(outs):
            ref[:block, cols] = v[i * block : (i + 1) * block, :].astype(ref.dtype)
        return carry

    lax.fori_loop(0, 4, tile, 0)
    for i, ref in enumerate(outs):
        m = jnp.broadcast_to(mass[:, i * block : (i + 1) * block], (EXTRA, block))
        r = m.astype(ref.dtype).astype(f32)
        m = jnp.where(line == 0, r, jnp.where(line == 1, m - r, 0.0)).astype(ref.dtype)
        ref[block:, :] = jnp.concatenate([m] * (width // block), axis=1)


def level_one_sums(index, e, factors, points):
    count, width = points[0].shape
    total = e[0].shape[0]
    block = total // 8
    types = [bf16] * 3 + [f32]
    vmem = pl.BlockSpec(memory_space=pltpu.VMEM)
    return pl.pallas_call(
        sums_kernel,
        in_specs=[pl.BlockSpec(memory_space=pltpu.SMEM)] + [HBM] * 2 + [vmem] * 2 + [HBM] * 2,
        out_specs=[vmem] * 4,
        scratch_shapes=[
            pltpu.VMEM((4 * block, 2 * count), bf16),
            pltpu.VMEM((4 * block, 128), f32),
            pltpu.VMEM((2, 4, block, count), bf16),
            pltpu.VMEM((2, count, width), bf16),
            pltpu.SemaphoreType.DMA((2, 4)),
            pltpu.SemaphoreType.DMA((2,)),
        ],
        out_shape=[jax.ShapeDtypeStruct((block + EXTRA, width), t) for t in types],
        compiler_params=pltpu.CompilerParams(vmem_limit_bytes=VMEM),
        cost_estimate=pl.CostEstimate(
            flops=2 * total * count * width,
            bytes_accessed=2 * count * (total + 2 * width) + 2 * total * width,
            transcendentals=0,
        ),
        name="level_one_sums",
    )(index, *map(far, e), *factors, *map(far, points))


def level_two_kernel(
    keep, place, rows_mine, rows_other, mass, table_far, *refs
):
    outs, (rows, turned, second, spread, table, sem) = refs[:8], refs[8:]
    block, width = rows_mine.shape
    count = table.shape[0]
    part = lambda i: pl.ds(pl.multiple_of(i * (count // 4), count // 4), count // 4)
    copy = lambda i: pltpu.make_async_copy(table_far.at[part(i), :], table.at[part(i), :], sem.at[i])
    for i in range(4):
        copy(i).start()
    rows[:block, :width] = rows_mine[...]
    rows[block:, :width] = rows_other[...]
    rows[:, width:] = jnp.ones((2 * block, 128), bf16)
    turned[...] = rows[:, :width].astype(f32).T.astype(bf16)

    def scores(i, high):
        copy(i).wait()
        at = part(i)
        wide = table[at, :].astype(f32)
        sq = jnp.sum(wide * wide, axis=1, keepdims=True) * sharp_two
        v = dot(table[at, :], turned[...], ((1,), (0,))) * (2.0 * sharp_two) - sq
        second[at, :] = v
        return jnp.maximum(high, jnp.max(v, axis=0, keepdims=True))

    high = lax.fori_loop(0, 4, scores, jnp.full((1, 2 * block), -jnp.inf, f32))

    def powers(i, total):
        v = jnp.exp(second[part(i), :] - high)
        second[part(i), :] = v
        return total + jnp.sum(v, axis=0, keepdims=True)

    total = lax.fori_loop(0, 4, powers, jnp.zeros((1, 2 * block), f32))
    weight = mass[...] / total
    half = width // 2
    lane = lax.broadcasted_iota(jnp.int32, (8 * 4 * keep, 128), 1)
    for i in range(4):
        for color in range(2):
            for j in range(4):
                to_x, to_y = (i, j) if color == 0 else (j, i)
                start = place[0] + (place[1 + to_x] * 32 + place[5 + to_y]) * keep
                starts = [start + (zh * 128 + zl * 4) * keep for zh in range(2) for zl in range(4)]
                v = [second[pl.ds(pl.multiple_of(s, keep), keep), :] for s in starts]
                to = slice(j * 8 * keep, (j + 1) * 8 * keep)
                spread[2 * i + color, to, :] = (jnp.concatenate(v) * weight).astype(bf16)
            cols = slice(0, half) if color == 0 else slice(half, width + 128)
            v = dot(spread[2 * i + color], rows[:, cols], ((1,), (0,)))
            out = outs[4 * color + i]
            if color == 0:
                out[...] = v.astype(out.dtype)
                continue
            r = v.astype(out.dtype)
            out[:, :half] = r[:, :half]
            left = (v[:, half:] - r[:, half:].astype(f32)).astype(out.dtype)
            out[:, half:] = jnp.where(lane > 0, left, r[:, half:])


def level_two_sums(place, rows_mine, rows_other, mass, table):
    block, width = rows_mine.shape
    count = table.shape[0]
    vmem = pl.BlockSpec(memory_space=pltpu.VMEM)
    return pl.pallas_call(
        functools.partial(level_two_kernel, count // 256),
        in_specs=[pl.BlockSpec(memory_space=pltpu.SMEM)] + [vmem] * 3 + [HBM],
        out_specs=[vmem] * 8,
        scratch_shapes=[
            pltpu.VMEM((2 * block, width + 128), bf16),
            pltpu.VMEM((width, 2 * block), bf16),
            pltpu.VMEM((count, 2 * block), f32),
            pltpu.VMEM((8, count // 8, 2 * block), bf16),
            pltpu.VMEM((count, width), bf16),
            pltpu.SemaphoreType.DMA((4,)),
        ],
        out_shape=[
            jax.ShapeDtypeStruct((count // 8, cols), t)
            for cols in (width // 2, width // 2 + 128)
            for t in (bf16, bf16, bf16, f32)
        ],
        compiler_params=pltpu.CompilerParams(vmem_limit_bytes=VMEM),
        cost_estimate=pl.CostEstimate(
            flops=8 * block * count * width,
            bytes_accessed=4 * count * width,
            transcendentals=2 * block * count,
        ),
        name="level_two_sums",
    )(place, rows_mine, rows_other, mass, far(table))


def on_device(points, cent_one, cent_two):
    width = points.shape[1]
    core, x, y, zh = [lax.axis_index(name) for name in ("core", "x", "y", "zh")]
    block = cent_one.shape[0] // 16

    scale = 0.5 * width ** (-0.5)

    with jax.named_scope("scores_one"):
        pts = (points, shift(points, "core", 2, 1))
        cents = lax.dynamic_slice_in_dim(cent_one, core * (8 * block), 8 * block, 0)
        sq = jnp.sum(jnp.square(cents.astype(f32)), axis=1)[:, None]

        def level_one_scores(p):
            scores = (2.0 * dot(cents, p, ((1,), (1,))) - sq) * scale
            high = jnp.max(scores, axis=0)
            e = jnp.exp(scores - high)
            return e.astype(bf16), high, high + jnp.log(jnp.sum(e, axis=0))

        first = level_one_scores(points)
        other, first = lax.optimization_barrier((pts[1], first))
        pts = (points, other)
        e, highs, sums = zip(first, level_one_scores(other))
    with jax.named_scope("exchange_softmax"):
        mine = log_total(jnp.stack([sums[0], shift(sums[1], "core", 2, 1)]))
        mine = log_total(swap(jnp.broadcast_to(mine, (16,) + mine.shape), CENT))
        norms = (mine, shift(mine, "core", 2, 1))
        factors = [jnp.exp(h - n)[None] for h, n in zip(highs, norms)]
    with jax.named_scope("reduce_one"):
        sums = []
        for z in (1 - zh, zh):
            index = ((x + jnp.array(HOPS, jnp.int32)) % 4) * 2 + z
            *sent, own = level_one_sums(index, e, factors, pts)
            got = [shift(v, "x", 4, k) for v, k in zip(sent, HOPS)]
            sums.append(own + sum(g.astype(f32) for g in got))
        part = sums[1] + lax.ppermute(with_mass(sums[0], block), "zh", [(0, 1), (1, 0)]).astype(f32)
    with jax.named_scope("finish_one"):
        mass = (part[block] + part[block + 1])[:block]
        place = ((core * 4 + x) * 2 + zh) * block
        old = lax.dynamic_slice_in_dim(cent_one, place, block, 0).astype(f32)
        rows = ((part[:block] + prior_one * old) / (mass[:, None] + prior_one)).astype(bf16)
        rows_other = shift(rows, "core", 2, 1)
        mass_all = jnp.stack([mass, shift(mass, "core", 2, 1)]).reshape(1, 2 * block)
    with jax.named_scope("scores_two"):
        keep = cent_two.shape[0] // 256
        hops = jnp.array(HOPS, jnp.int32)
        place = jnp.concatenate([(core * 16 * keep).reshape(1), (x + hops) % 4, (y + hops) % 4])
        parts = level_two_sums(place, rows, rows_other, mass_all, cent_two)
    with jax.named_scope("reduce_two"):
        half = width // 2
        size = 8 * keep

        def gather(parts, axis):
            got = [shift(v, axis, 4, k) for v, k in zip(parts[:3], HOPS)]
            return parts[3] + sum(g.astype(f32) for g in got)

        one, two = gather(parts[:4], "x"), gather(parts[4:], "y")
        cut = lambda v: [v[i * size : (i + 1) * size] for i in range(3)]
        one = gather(cut(one.astype(bf16)) + [one[3 * size :]], "y")
        two = gather(cut(with_mass_columns(two, half)) + [two[3 * size :]], "x")
        part = wide = jnp.concatenate([one, two], axis=1)
        part = jnp.sum(swap(part, ("zh", "zl")).reshape(8, keep, width + 128), axis=0)
        mass = part[:, width : width + 1] + part[:, width + 1 : width + 2]
    with jax.named_scope("out_one"):
        mine = [
            lax.dynamic_index_in_dim(r.reshape(block, 2, 4, 2, width // 16), core, 3, False)
            for r in (rows, rows_other)
        ]
        both = jnp.where(core == 0, jnp.stack(mine), jnp.stack(mine[::-1]))
        both = both.transpose(2, 3, 0, 1, 4)
        stay = lax.dynamic_index_in_dim(both, zh, 0, False)
        go = lax.dynamic_index_in_dim(both, 1 - zh, 0, False)
        come = lax.ppermute(go, "zh", [(0, 1), (1, 0)])
        pair = jnp.where(zh == 0, jnp.stack([stay, come]), jnp.stack([come, stay]))
        pair = pair.transpose(1, 0, 2, 3, 4)
        by_x = [lax.dynamic_index_in_dim(pair, (x + k) % 4, 0, False) for k in range(4)]
        by_x, _ = lax.optimization_barrier((by_x, wide))
        by_x = jnp.stack([by_x[0]] + [shift(by_x[k], "x", 4, k) for k in (1, 2, 3)])
        by_x = jnp.roll(by_x[::-1], x + 1, axis=0)
        new_one = by_x.transpose(2, 0, 1, 3, 4).reshape(16 * block, width // 16)
    with jax.named_scope("finish_two"):
        place = lax.axis_index(ALL)
        old = lax.dynamic_slice_in_dim(cent_two, place * keep, keep, 0).astype(f32)
        new_two = ((part[:, :width] + prior_two * old) / (mass + prior_two)).astype(bf16)
    return (new_one, new_two)


def solution(mesh):
    inner = Mesh(mesh.devices.reshape(2, 4, 2, 4, 4), ALL)
    dp = ("zh", "x", "core")
    in_specs = (P(dp, None), P(CENT, None), P())
    out_specs = (P(CENT, dp), P(ALL, None))
    return jax.shard_map(
        on_device, mesh=inner, in_specs=in_specs, out_specs=out_specs, check_vma=False
    )
```

```python
import functools

import jax
import jax.numpy as jnp
from jax import lax
from jax.experimental import pallas as pl
from jax.experimental.pallas import tpu as pltpu
from jax.sharding import Mesh, PartitionSpec as P

prior_one = 0.5
prior_two = 2.0
sharp_two = 0.25

CENT = ("zl", "y")
ALL = ("zh", "x", "core", "zl", "y")
HOPS = (2, 1, 3, 0)
EXTRA = 16
VMEM = 32 * 2**20
HBM = pl.BlockSpec(memory_space=pltpu.HBM)
f32 = jnp.float32
bf16 = jnp.bfloat16


def swap(v, axis):
    return lax.all_to_all(v, axis, 0, 0, tiled=True)


def shift(v, axis, n, k):
    return lax.ppermute(v, axis, [(i, (i + k) % n) for i in range(n)])


def far(v):
    return pltpu.with_memory_space_constraint(v, pltpu.HBM)


def dot(a, b, dims):
    return lax.dot_general(a, b, (dims, ((), ())), preferred_element_type=f32)


def with_mass(v, block):
    mass = v[block : block + 1] + v[block + 1 : block + 2]
    rounded = lax.reduce_precision(mass, 8, 7)
    line = lax.broadcasted_iota(jnp.int32, v.shape, 0)
    v = jnp.where(line == block, rounded, jnp.where(line == block + 1, mass - rounded, v))
    return v.astype(bf16)


def with_mass_columns(v, half):
    mass = v[:, half : half + 1] + v[:, half + 1 : half + 2]
    rounded = lax.reduce_precision(mass, 8, 7)
    lane = lax.broadcasted_iota(jnp.int32, v.shape, 1)
    v = jnp.where(lane == half, rounded, jnp.where(lane > half, mass - rounded, v))
    return v.astype(bf16)


def log_total(scores):
    high = jnp.max(scores, axis=0)
    return high + jnp.log(jnp.sum(jnp.exp(scores - high), axis=0))


def sums_kernel(index, e_mine, e_other, f_mine, f_other, p_mine, p_other, *refs):
    outs, (weights, lanes, e_held, p_held, e_sem, p_sem) = refs[:4], refs[4:]
    block = outs[0].shape[0] - EXTRA
    count, width = p_mine.shape
    def e_copy(i, j, e):
        at = pl.ds(pl.multiple_of(index[i] * block, block), block)
        return pltpu.make_async_copy(e.at[at, :], e_held.at[j, i], e_sem.at[j, i])

    def p_copy(n, j, p):
        at = pl.ds(pl.multiple_of(n * (width // 4), width // 4), width // 4)
        return pltpu.make_async_copy(p.at[:, at], p_held.at[j, :, at], p_sem.at[j, n])

    for i in range(4):
        for j, e in enumerate((e_mine, e_other)):
            e_copy(i, j, e).start()
    for n in range(4):
        for j, p in enumerate((p_mine, p_other)):
            p_copy(n, j, p).start()

    def fill(i, carry):
        to = pl.ds(pl.multiple_of(i * block, block), block)
        lane = 0.0
        for j, (e, f) in enumerate(((e_mine, f_mine), (e_other, f_other))):
            e_copy(i, j, e).wait()
            w = e_held[j, i].astype(f32) * f[...]
            for n in range(count // 128):
                lane = lane + w[:, n * 128 : (n + 1) * 128]
            weights[to, j * count : (j + 1) * count] = w.astype(bf16)
        lanes[to, :] = lane
        return carry

    lax.fori_loop(0, 4, fill, 0)
    mass = jnp.sum(lanes[...].T, axis=0, keepdims=True)
    line = lax.broadcasted_iota(jnp.int32, (EXTRA, block), 0)

    def tile(n, carry):
        cols = pl.ds(pl.multiple_of(n * (width // 4), width // 4), width // 4)
        for j, p in enumerate((p_mine, p_other)):
            p_copy(n, j, p).wait()
        v = dot(weights[:, :count], p_held[0, :, cols], ((1,), (0,)))
        v += dot(weights[:, count:], p_held[1, :, cols], ((1,), (0,)))
        for i, ref in enumerate(outs):
            ref[:block, cols] = v[i * block : (i + 1) * block, :].astype(ref.dtype)
        return carry

    lax.fori_loop(0, 4, tile, 0)
    for i, ref in enumerate(outs):
        m = jnp.broadcast_to(mass[:, i * block : (i + 1) * block], (EXTRA, block))
        r = m.astype(ref.dtype).astype(f32)
        m = jnp.where(line == 0, r, jnp.where(line == 1, m - r, 0.0)).astype(ref.dtype)
        ref[block:, :] = jnp.concatenate([m] * (width // block), axis=1)


def level_one_sums(index, e, factors, points):
    count, width = points[0].shape
    total = e[0].shape[0]
    block = total // 8
    types = [bf16] * 3 + [f32]
    vmem = pl.BlockSpec(memory_space=pltpu.VMEM)
    return pl.pallas_call(
        sums_kernel,
        in_specs=[pl.BlockSpec(memory_space=pltpu.SMEM)] + [HBM] * 2 + [vmem] * 2 + [HBM] * 2,
        out_specs=[vmem] * 4,
        scratch_shapes=[
            pltpu.VMEM((4 * block, 2 * count), bf16),
            pltpu.VMEM((4 * block, 128), f32),
            pltpu.VMEM((2, 4, block, count), bf16),
            pltpu.VMEM((2, count, width), bf16),
            pltpu.SemaphoreType.DMA((2, 4)),
            pltpu.SemaphoreType.DMA((2, 4)),
        ],
        out_shape=[jax.ShapeDtypeStruct((block + EXTRA, width), t) for t in types],
        compiler_params=pltpu.CompilerParams(vmem_limit_bytes=VMEM),
        cost_estimate=pl.CostEstimate(
            flops=2 * total * count * width,
            bytes_accessed=2 * count * (total + 2 * width) + 2 * total * width,
            transcendentals=0,
        ),
        name="level_one_sums",
    )(index, *map(far, e), *factors, *map(far, points))


def level_two_kernel(
    keep, place, rows_mine, rows_other, mass, table_far, *refs
):
    outs, (rows, turned, second, spread, table, sem) = refs[:8], refs[8:]
    block, width = rows_mine.shape
    count = table.shape[0]
    part = lambda i: pl.ds(pl.multiple_of(i * (count // 4), count // 4), count // 4)
    copy = lambda i: pltpu.make_async_copy(table_far.at[part(i), :], table.at[part(i), :], sem.at[i])
    for i in range(4):
        copy(i).start()
    rows[:block, :width] = rows_mine[...]
    rows[block:, :width] = rows_other[...]
    rows[:, width:] = jnp.ones((2 * block, 128), bf16)
    turned[...] = rows[:, :width].astype(f32).T.astype(bf16)

    def scores(i, high):
        copy(i).wait()
        at = part(i)
        wide = table[at, :].astype(f32)
        sq = jnp.sum(wide * wide, axis=1, keepdims=True) * sharp_two
        v = dot(table[at, :], turned[...], ((1,), (0,))) * (2.0 * sharp_two) - sq
        second[at, :] = v
        return jnp.maximum(high, jnp.max(v, axis=0, keepdims=True))

    high = lax.fori_loop(0, 4, scores, jnp.full((1, 2 * block), -jnp.inf, f32))

    def powers(i, total):
        v = jnp.exp(second[part(i), :] - high)
        second[part(i), :] = v
        return total + jnp.sum(v, axis=0, keepdims=True)

    total = lax.fori_loop(0, 4, powers, jnp.zeros((1, 2 * block), f32))
    weight = mass[...] / total
    half = width // 2
    lane = lax.broadcasted_iota(jnp.int32, (8 * 4 * keep, 128), 1)
    for i in range(4):
        for color in range(2):
            for j in range(4):
                to_x, to_y = (i, j) if color == 0 else (j, i)
                start = place[0] + (place[1 + to_x] * 32 + place[5 + to_y]) * keep
                starts = [start + (zh * 128 + zl * 4) * keep for zh in range(2) for zl in range(4)]
                v = [second[pl.ds(pl.multiple_of(s, keep), keep), :] for s in starts]
                to = slice(j * 8 * keep, (j + 1) * 8 * keep)
                spread[2 * i + color, to, :] = (jnp.concatenate(v) * weight).astype(bf16)
            cols = slice(0, half) if color == 0 else slice(half, width + 128)
            v = dot(spread[2 * i + color], rows[:, cols], ((1,), (0,)))
            out = outs[4 * color + i]
            if color == 0:
                out[...] = v.astype(out.dtype)
                continue
            r = v.astype(out.dtype)
            out[:, :half] = r[:, :half]
            left = (v[:, half:] - r[:, half:].astype(f32)).astype(out.dtype)
            out[:, half:] = jnp.where(lane > 0, left, r[:, half:])


def level_two_sums(place, rows_mine, rows_other, mass, table):
    block, width = rows_mine.shape
    count = table.shape[0]
    vmem = pl.BlockSpec(memory_space=pltpu.VMEM)
    return pl.pallas_call(
        functools.partial(level_two_kernel, count // 256),
        in_specs=[pl.BlockSpec(memory_space=pltpu.SMEM)] + [vmem] * 3 + [HBM],
        out_specs=[vmem] * 8,
        scratch_shapes=[
            pltpu.VMEM((2 * block, width + 128), bf16),
            pltpu.VMEM((width, 2 * block), bf16),
            pltpu.VMEM((count, 2 * block), f32),
            pltpu.VMEM((8, count // 8, 2 * block), bf16),
            pltpu.VMEM((count, width), bf16),
            pltpu.SemaphoreType.DMA((4,)),
        ],
        out_shape=[
            jax.ShapeDtypeStruct((count // 8, cols), t)
            for cols in (width // 2, width // 2 + 128)
            for t in (bf16, bf16, bf16, f32)
        ],
        compiler_params=pltpu.CompilerParams(vmem_limit_bytes=VMEM),
        cost_estimate=pl.CostEstimate(
            flops=8 * block * count * width,
            bytes_accessed=4 * count * width,
            transcendentals=2 * block * count,
        ),
        name="level_two_sums",
    )(place, rows_mine, rows_other, mass, far(table))


def on_device(points, cent_one, cent_two):
    width = points.shape[1]
    core, x, y, zh = [lax.axis_index(name) for name in ("core", "x", "y", "zh")]
    block = cent_one.shape[0] // 16

    scale = 0.5 * width ** (-0.5)

    with jax.named_scope("scores_one"):
        pts = (points, shift(points, "core", 2, 1))
        cents = lax.dynamic_slice_in_dim(cent_one, core * (8 * block), 8 * block, 0)
        sq = jnp.sum(jnp.square(cents.astype(f32)), axis=1)[:, None]

        def level_one_scores(p):
            scores = (2.0 * dot(cents, p, ((1,), (1,))) - sq) * scale
            high = jnp.max(scores, axis=0)
            e = jnp.exp(scores - high)
            return e.astype(bf16), high, high + jnp.log(jnp.sum(e, axis=0))

        first = level_one_scores(points)
        other, first = lax.optimization_barrier((pts[1], first))
        pts = (points, other)
        e, highs, sums = zip(first, level_one_scores(other))
    with jax.named_scope("exchange_softmax"):
        mine = log_total(jnp.stack([sums[0], shift(sums[1], "core", 2, 1)]))
        mine = log_total(swap(jnp.broadcast_to(mine, (16,) + mine.shape), CENT))
        norms = (mine, shift(mine, "core", 2, 1))
        factors = [jnp.exp(h - n)[None] for h, n in zip(highs, norms)]
    with jax.named_scope("reduce_one"):
        sums = []
        for z in (1 - zh, zh):
            index = ((x + jnp.array(HOPS, jnp.int32)) % 4) * 2 + z
            *sent, own = level_one_sums(index, e, factors, pts)
            got = [shift(v, "x", 4, k) for v, k in zip(sent, HOPS)]
            sums.append(own + sum(g.astype(f32) for g in got))
        part = sums[1] + lax.ppermute(with_mass(sums[0], block), "zh", [(0, 1), (1, 0)]).astype(f32)
    with jax.named_scope("finish_one"):
        mass = (part[block] + part[block + 1])[:block]
        place = ((core * 4 + x) * 2 + zh) * block
        old = lax.dynamic_slice_in_dim(cent_one, place, block, 0).astype(f32)
        rows = ((part[:block] + prior_one * old) / (mass[:, None] + prior_one)).astype(bf16)
        rows_other = shift(rows, "core", 2, 1)
        mass_all = jnp.stack([mass, shift(mass, "core", 2, 1)]).reshape(1, 2 * block)
    with jax.named_scope("scores_two"):
        keep = cent_two.shape[0] // 256
        hops = jnp.array(HOPS, jnp.int32)
        place = jnp.concatenate([(core * 16 * keep).reshape(1), (x + hops) % 4, (y + hops) % 4])
        parts = level_two_sums(place, rows, rows_other, mass_all, cent_two)
    with jax.named_scope("reduce_two"):
        half = width // 2
        size = 8 * keep

        def gather(parts, axis):
            got = [shift(v, axis, 4, k) for v, k in zip(parts[:3], HOPS)]
            return parts[3] + sum(g.astype(f32) for g in got)

        one, two = gather(parts[:4], "x"), gather(parts[4:], "y")
        cut = lambda v: [v[i * size : (i + 1) * size] for i in range(3)]
        one = gather(cut(one.astype(bf16)) + [one[3 * size :]], "y")
        two = gather(cut(with_mass_columns(two, half)) + [two[3 * size :]], "x")
        part = wide = jnp.concatenate([one, two], axis=1)
        part = jnp.sum(swap(part, ("zh", "zl")).reshape(8, keep, width + 128), axis=0)
        mass = part[:, width : width + 1] + part[:, width + 1 : width + 2]
    with jax.named_scope("out_one"):
        mine = [
            lax.dynamic_index_in_dim(r.reshape(block, 2, 4, 2, width // 16), core, 3, False)
            for r in (rows, rows_other)
        ]
        both = jnp.where(core == 0, jnp.stack(mine), jnp.stack(mine[::-1]))
        both = both.transpose(2, 3, 0, 1, 4)
        stay = lax.dynamic_index_in_dim(both, zh, 0, False)
        go = lax.dynamic_index_in_dim(both, 1 - zh, 0, False)
        come = lax.ppermute(go, "zh", [(0, 1), (1, 0)])
        pair = jnp.where(zh == 0, jnp.stack([stay, come]), jnp.stack([come, stay]))
        pair = pair.transpose(1, 0, 2, 3, 4)
        by_x = [lax.dynamic_index_in_dim(pair, (x + k) % 4, 0, False) for k in range(4)]
        by_x, _ = lax.optimization_barrier((by_x, wide))
        by_x = jnp.stack([by_x[0]] + [shift(by_x[k], "x", 4, k) for k in (1, 2, 3)])
        by_x = jnp.roll(by_x[::-1], x + 1, axis=0)
        new_one = by_x.transpose(2, 0, 1, 3, 4).reshape(16 * block, width // 16)
    with jax.named_scope("finish_two"):
        place = lax.axis_index(ALL)
        old = lax.dynamic_slice_in_dim(cent_two, place * keep, keep, 0).astype(f32)
        new_two = ((part[:, :width] + prior_two * old) / (mass + prior_two)).astype(bf16)
    return (new_one, new_two)


def solution(mesh):
    inner = Mesh(mesh.devices.reshape(2, 4, 2, 4, 4), ALL)
    dp = ("zh", "x", "core")
    in_specs = (P(dp, None), P(CENT, None), P())
    out_specs = (P(CENT, dp), P(ALL, None))
    return jax.shard_map(
        on_device, mesh=inner, in_specs=in_specs, out_specs=out_specs, check_vma=False
    )
```

```python
import functools

import jax
import jax.numpy as jnp
from jax import lax
from jax.experimental import pallas as pl
from jax.experimental.pallas import tpu as pltpu
from jax.sharding import Mesh, PartitionSpec as P

prior_one = 0.5
prior_two = 2.0
sharp_two = 0.25

CENT = ("zl", "y")
ALL = ("zh", "x", "core", "zl", "y")
HOPS = (2, 1, 3, 0)
EXTRA = 16
VMEM = 32 * 2**20
HBM = pl.BlockSpec(memory_space=pltpu.HBM)
f32 = jnp.float32
bf16 = jnp.bfloat16


def swap(v, axis):
    return lax.all_to_all(v, axis, 0, 0, tiled=True)


def shift(v, axis, n, k):
    return lax.ppermute(v, axis, [(i, (i + k) % n) for i in range(n)])


def far(v):
    return pltpu.with_memory_space_constraint(v, pltpu.HBM)


def dot(a, b, dims):
    return lax.dot_general(a, b, (dims, ((), ())), preferred_element_type=f32)


def with_mass(v, block):
    mass = v[block : block + 1] + v[block + 1 : block + 2]
    rounded = lax.reduce_precision(mass, 8, 7)
    line = lax.broadcasted_iota(jnp.int32, v.shape, 0)
    v = jnp.where(line == block, rounded, jnp.where(line == block + 1, mass - rounded, v))
    return v.astype(bf16)


def with_mass_columns(v, half):
    mass = v[:, half : half + 1] + v[:, half + 1 : half + 2]
    rounded = lax.reduce_precision(mass, 8, 7)
    lane = lax.broadcasted_iota(jnp.int32, v.shape, 1)
    v = jnp.where(lane == half, rounded, jnp.where(lane > half, mass - rounded, v))
    return v.astype(bf16)


def log_total(scores):
    high = jnp.max(scores, axis=0)
    return high + jnp.log(jnp.sum(jnp.exp(scores - high), axis=0))


def sums_kernel(index, e_mine, e_other, f_mine, f_other, p_mine, p_other, *refs):
    outs, (weights, lanes, e_held, p_held, e_sem, p_sem) = refs[:4], refs[4:]
    block = outs[0].shape[0] - EXTRA
    count, width = p_mine.shape
    def e_copy(i, j, e):
        at = pl.ds(pl.multiple_of(index[i] * block, block), block)
        return pltpu.make_async_copy(e.at[at, :], e_held.at[j, i], e_sem.at[j, i])

    p_copies = [
        pltpu.make_async_copy(p, p_held.at[j * count : (j + 1) * count, :], p_sem.at[j]) for j, p in enumerate((p_mine, p_other))
    ]
    for i in range(4):
        for j, e in enumerate((e_mine, e_other)):
            e_copy(i, j, e).start()
    for copy in p_copies:
        copy.start()

    def fill(i, carry):
        to = pl.ds(pl.multiple_of(i * block, block), block)
        lane = 0.0
        for j, (e, f) in enumerate(((e_mine, f_mine), (e_other, f_other))):
            e_copy(i, j, e).wait()
            w = e_held[j, i].astype(f32) * f[...]
            for n in range(count // 128):
                lane = lane + w[:, n * 128 : (n + 1) * 128]
            weights[to, j * count : (j + 1) * count] = w.astype(bf16)
        lanes[to, :] = lane
        return carry

    lax.fori_loop(0, 4, fill, 0)
    mass = jnp.sum(lanes[...].T, axis=0, keepdims=True)
    line = lax.broadcasted_iota(jnp.int32, (EXTRA, block), 0)
    for copy in p_copies:
        copy.wait()

    def tile(n, carry):
        cols = pl.ds(pl.multiple_of(n * (width // 4), width // 4), width // 4)
        v = dot(weights[...], p_held[:, cols], ((1,), (0,)))
        for i, ref in enumerate(outs):
            ref[:block, cols] = v[i * block : (i + 1) * block, :].astype(ref.dtype)
        return carry

    lax.fori_loop(0, 4, tile, 0)
    for i, ref in enumerate(outs):
        m = jnp.broadcast_to(mass[:, i * block : (i + 1) * block], (EXTRA, block))
        r = m.astype(ref.dtype).astype(f32)
        m = jnp.where(line == 0, r, jnp.where(line == 1, m - r, 0.0)).astype(ref.dtype)
        ref[block:, :] = jnp.concatenate([m] * (width // block), axis=1)


def level_one_sums(index, e, factors, points):
    count, width = points[0].shape
    total = e[0].shape[0]
    block = total // 8
    types = [bf16] * 3 + [f32]
    vmem = pl.BlockSpec(memory_space=pltpu.VMEM)
    return pl.pallas_call(
        sums_kernel,
        in_specs=[pl.BlockSpec(memory_space=pltpu.SMEM)] + [HBM] * 2 + [vmem] * 2 + [HBM] * 2,
        out_specs=[vmem] * 4,
        scratch_shapes=[
            pltpu.VMEM((4 * block, 2 * count), bf16),
            pltpu.VMEM((4 * block, 128), f32),
            pltpu.VMEM((2, 4, block, count), bf16),
            pltpu.VMEM((2 * count, width), bf16),
            pltpu.SemaphoreType.DMA((2, 4)),
            pltpu.SemaphoreType.DMA((2,)),
        ],
        out_shape=[jax.ShapeDtypeStruct((block + EXTRA, width), t) for t in types],
        compiler_params=pltpu.CompilerParams(vmem_limit_bytes=VMEM),
        cost_estimate=pl.CostEstimate(
            flops=2 * total * count * width,
            bytes_accessed=2 * count * (total + 2 * width) + 2 * total * width,
            transcendentals=0,
        ),
        name="level_one_sums",
    )(index, *map(far, e), *factors, *map(far, points))


def level_two_kernel(
    keep, place, rows_mine, rows_other, mass, table_far, *refs
):
    outs, (rows, turned, second, spread, table, sem) = refs[:8], refs[8:]
    block, width = rows_mine.shape
    count = table.shape[0]
    part = lambda i: pl.ds(pl.multiple_of(i * (count // 4), count // 4), count // 4)
    copy = lambda i: pltpu.make_async_copy(table_far.at[part(i), :], table.at[part(i), :], sem.at[i])
    for i in range(4):
        copy(i).start()
    rows[:block, :width] = rows_mine[...]
    rows[block:, :width] = rows_other[...]
    rows[:, width:] = jnp.ones((2 * block, 128), bf16)
    turned[...] = rows[:, :width].astype(f32).T.astype(bf16)

    def scores(i, high):
        copy(i).wait()
        at = part(i)
        wide = table[at, :].astype(f32)
        sq = jnp.sum(wide * wide, axis=1, keepdims=True) * sharp_two
        v = dot(table[at, :], turned[...], ((1,), (0,))) * (2.0 * sharp_two) - sq
        second[at, :] = v
        return jnp.maximum(high, jnp.max(v, axis=0, keepdims=True))

    high = lax.fori_loop(0, 4, scores, jnp.full((1, 2 * block), -jnp.inf, f32))

    def powers(i, total):
        v = jnp.exp(second[part(i), :] - high)
        second[part(i), :] = v
        return total + jnp.sum(v, axis=0, keepdims=True)

    total = lax.fori_loop(0, 4, powers, jnp.zeros((1, 2 * block), f32))
    weight = mass[...] / total
    half = width // 2
    lane = lax.broadcasted_iota(jnp.int32, (8 * 4 * keep, 128), 1)
    for i in range(4):
        for color in range(2):
            for j in range(4):
                to_x, to_y = (i, j) if color == 0 else (j, i)
                start = place[0] + (place[1 + to_x] * 32 + place[5 + to_y]) * keep
                starts = [start + (zh * 128 + zl * 4) * keep for zh in range(2) for zl in range(4)]
                v = [second[pl.ds(pl.multiple_of(s, keep), keep), :] for s in starts]
                to = slice(j * 8 * keep, (j + 1) * 8 * keep)
                spread[2 * i + color, to, :] = (jnp.concatenate(v) * weight).astype(bf16)
            cols = slice(0, half) if color == 0 else slice(half, width + 128)
            v = dot(spread[2 * i + color], rows[:, cols], ((1,), (0,)))
            out = outs[4 * color + i]
            if color == 0:
                out[...] = v.astype(out.dtype)
                continue
            r = v.astype(out.dtype)
            out[:, :half] = r[:, :half]
            left = (v[:, half:] - r[:, half:].astype(f32)).astype(out.dtype)
            out[:, half:] = jnp.where(lane > 0, left, r[:, half:])


def level_two_sums(place, rows_mine, rows_other, mass, table):
    block, width = rows_mine.shape
    count = table.shape[0]
    vmem = pl.BlockSpec(memory_space=pltpu.VMEM)
    return pl.pallas_call(
        functools.partial(level_two_kernel, count // 256),
        in_specs=[pl.BlockSpec(memory_space=pltpu.SMEM)] + [vmem] * 3 + [HBM],
        out_specs=[vmem] * 8,
        scratch_shapes=[
            pltpu.VMEM((2 * block, width + 128), bf16),
            pltpu.VMEM((width, 2 * block), bf16),
            pltpu.VMEM((count, 2 * block), f32),
            pltpu.VMEM((8, count // 8, 2 * block), bf16),
            pltpu.VMEM((count, width), bf16),
            pltpu.SemaphoreType.DMA((4,)),
        ],
        out_shape=[
            jax.ShapeDtypeStruct((count // 8, cols), t)
            for cols in (width // 2, width // 2 + 128)
            for t in (bf16, bf16, bf16, f32)
        ],
        compiler_params=pltpu.CompilerParams(vmem_limit_bytes=VMEM),
        cost_estimate=pl.CostEstimate(
            flops=8 * block * count * width,
            bytes_accessed=4 * count * width,
            transcendentals=2 * block * count,
        ),
        name="level_two_sums",
    )(place, rows_mine, rows_other, mass, far(table))


def on_device(points, cent_one, cent_two):
    width = points.shape[1]
    core, x, y, zh = [lax.axis_index(name) for name in ("core", "x", "y", "zh")]
    block = cent_one.shape[0] // 16

    scale = 0.5 * width ** (-0.5)

    with jax.named_scope("scores_one"):
        pts = (points, shift(points, "core", 2, 1))
        cents = lax.dynamic_slice_in_dim(cent_one, core * (8 * block), 8 * block, 0)
        sq = jnp.sum(jnp.square(cents.astype(f32)), axis=1)[:, None]

        def level_one_scores(p):
            scores = (2.0 * dot(cents, p, ((1,), (1,))) - sq) * scale
            high = jnp.max(scores, axis=0)
            e = jnp.exp(scores - high)
            return e.astype(bf16), high, high + jnp.log(jnp.sum(e, axis=0))

        first = level_one_scores(points)
        other, first = lax.optimization_barrier((pts[1], first))
        pts = (points, other)
        e, highs, sums = zip(first, level_one_scores(other))
    with jax.named_scope("exchange_softmax"):
        mine = log_total(jnp.stack([sums[0], shift(sums[1], "core", 2, 1)]))
        mine = log_total(swap(jnp.broadcast_to(mine, (16,) + mine.shape), CENT))
        norms = (mine, shift(mine, "core", 2, 1))
        factors = [jnp.exp(h - n)[None] for h, n in zip(highs, norms)]
    with jax.named_scope("reduce_one"):
        sums = []
        for z in (1 - zh, zh):
            index = ((x + jnp.array(HOPS, jnp.int32)) % 4) * 2 + z
            *sent, own = level_one_sums(index, e, factors, pts)
            got = [shift(v, "x", 4, k) for v, k in zip(sent, HOPS)]
            sums.append(own + sum(g.astype(f32) for g in got))
        part = sums[1] + lax.ppermute(with_mass(sums[0], block), "zh", [(0, 1), (1, 0)]).astype(f32)
    with jax.named_scope("finish_one"):
        mass = (part[block] + part[block + 1])[:block]
        place = ((core * 4 + x) * 2 + zh) * block
        old = lax.dynamic_slice_in_dim(cent_one, place, block, 0).astype(f32)
        rows = ((part[:block] + prior_one * old) / (mass[:, None] + prior_one)).astype(bf16)
        rows_other = shift(rows, "core", 2, 1)
        mass_all = jnp.stack([mass, shift(mass, "core", 2, 1)]).reshape(1, 2 * block)
    with jax.named_scope("scores_two"):
        keep = cent_two.shape[0] // 256
        hops = jnp.array(HOPS, jnp.int32)
        place = jnp.concatenate([(core * 16 * keep).reshape(1), (x + hops) % 4, (y + hops) % 4])
        parts = level_two_sums(place, rows, rows_other, mass_all, cent_two)
    with jax.named_scope("reduce_two"):
        half = width // 2
        size = 8 * keep

        def gather(parts, axis):
            got = [shift(v, axis, 4, k) for v, k in zip(parts[:3], HOPS)]
            return parts[3] + sum(g.astype(f32) for g in got)

        one, two = gather(parts[:4], "x"), gather(parts[4:], "y")
        cut = lambda v: [v[i * size : (i + 1) * size] for i in range(3)]
        one = gather(cut(one.astype(bf16)) + [one[3 * size :]], "y")
        two = gather(cut(with_mass_columns(two, half)) + [two[3 * size :]], "x")
        part = wide = jnp.concatenate([one, two], axis=1)
        part = jnp.sum(swap(part, ("zh", "zl")).reshape(8, keep, width + 128), axis=0)
        mass = part[:, width : width + 1] + part[:, width + 1 : width + 2]
    with jax.named_scope("out_one"):
        mine = [
            lax.dynamic_index_in_dim(r.reshape(block, 2, 4, 2, width // 16), core, 3, False)
            for r in (rows, rows_other)
        ]
        both = jnp.where(core == 0, jnp.stack(mine), jnp.stack(mine[::-1]))
        both = both.transpose(2, 3, 0, 1, 4)
        stay = lax.dynamic_index_in_dim(both, zh, 0, False)
        go = lax.dynamic_index_in_dim(both, 1 - zh, 0, False)
        come = lax.ppermute(go, "zh", [(0, 1), (1, 0)])
        pair = jnp.where(zh == 0, jnp.stack([stay, come]), jnp.stack([come, stay]))
        pair = pair.transpose(1, 0, 2, 3, 4)
        by_x = [lax.dynamic_index_in_dim(pair, (x + k) % 4, 0, False) for k in range(4)]
        by_x, _ = lax.optimization_barrier((by_x, wide))
        by_x = jnp.stack([by_x[0]] + [shift(by_x[k], "x", 4, k) for k in (1, 2, 3)])
        by_x = jnp.roll(by_x[::-1], x + 1, axis=0)
        new_one = by_x.transpose(2, 0, 1, 3, 4).reshape(16 * block, width // 16)
    with jax.named_scope("finish_two"):
        place = lax.axis_index(ALL)
        old = lax.dynamic_slice_in_dim(cent_two, place * keep, keep, 0).astype(f32)
        new_two = ((part[:, :width] + prior_two * old) / (mass + prior_two)).astype(bf16)
    return (new_one, new_two)


def solution(mesh):
    inner = Mesh(mesh.devices.reshape(2, 4, 2, 4, 4), ALL)
    dp = ("zh", "x", "core")
    in_specs = (P(dp, None), P(CENT, None), P())
    out_specs = (P(CENT, dp), P(ALL, None))
    return jax.shard_map(
        on_device, mesh=inner, in_specs=in_specs, out_specs=out_specs, check_vma=False
    )
```
